32 devices in a mesh: section: 16 (over z, y, core), dp: 2 (over x).
Axes of the slice: x: 2, y: 2, z: 4, core: 2. Of those that a mesh axis runs over, the one named last changes fastest.
Arguments:
- fwd_h: bfloat16 [16, 256, 2048], P('section', None, 'dp'), may hold values from -6 to 6
- fwd_mem: bfloat16 [16, 256, 2048], P('section', None, 'dp'), may hold values from -6 to 6
- saved_h: bfloat16 [16, 256, 2048], P('section', None, 'dp'), may hold values from -6 to 6
- saved_mem: bfloat16 [16, 256, 2048], P('section', None, 'dp'), may hold values from -6 to 6
- back_h: bfloat16 [16, 256, 2048], P('section', None, 'dp'), may hold values from -6 to 6
- back_mem: bfloat16 [16, 256, 2048], P('section', None, 'dp'), may hold values from -6 to 6
- weight: bfloat16 [16, 2048, 2048], P('section', None, 'dp'), may hold values from -0.125 to 0.125
- row_stat: float32 [16, 2048], P('section'), may hold values from 0.05 to 5
- col_stat: float32 [16, 2048], P('section', 'dp'), may hold values from 0.05 to 5
- enc_count: int32 [1], replicated, may hold values from 4 to 12
- target_embed: bfloat16 [256, 2048], P(None, 'dp'), may hold values from -6 to 6
Outputs:
- next_h: bfloat16 [16, 256, 2048], P('section', None, 'dp')
- next_mem: bfloat16 [16, 256, 2048], P('section', None, 'dp')
- prev_h: bfloat16 [16, 256, 2048], P('section', None, 'dp')
- prev_mem: bfloat16 [16, 256, 2048], P('section', None, 'dp')
- update: bfloat16 [16, 2048, 2048], P('section', None, 'dp')
- row_new: float32 [16, 2048], P('section')
- col_new: float32 [16, 2048], P('section', 'dp')
The draws below stay inside these ranges and needn't reach their ends.
Inputs may be any that keep to these rules, and one draw needn't show every extreme that they name: Sections 0 to enc_count - 1 are encoder sections, the others decoder sections.
All inputs are finite; a program needn't handle non-finite values.
Results may differ from the reference program's by a relative error of at most 0.0086.
Values may be sent and summed in bfloat16 or wider, within the bound.
A program may use at most 128 MiB of HBM per device.

```python
import math
import jax
import jax.numpy as jnp
from jax import lax

D = 2048
HEADS = 8
HD = 256
ROWS = 256
INNER = 2048
N_SECTION = 16
N_DP = 2


def levels(own_key, dims, shards, least, largest):
    gain, own = 1.0, jax.random.fold_in(own_key, 6)
    for dim, blocks in shards:
        steps = jnp.exp(jax.random.uniform(jax.random.fold_in(own, dim), (blocks,), jnp.float32, least / len(shards), largest / len(shards)))
        gain = gain * jnp.repeat(steps, dims[dim] // blocks).reshape([-1 if axis == dim else 1 for axis in range(len(dims))])
    return gain


def scatter_about(key, shape, scale, bound, cuts=(), kind=jnp.bfloat16):
    gain = levels(key, shape, cuts, -0.22, 0.18) if cuts else 1.0
    values = jax.random.normal(key, shape, jnp.float32) * scale * gain
    return jnp.minimum(jnp.maximum(values, -bound), bound).astype(kind)


def setup_inputs(seed: int = 0) -> dict:
    arg_keys = jax.random.split(jax.random.key(seed), 12)
    fwd_h = scatter_about(arg_keys[0], (N_SECTION, ROWS, D), 1.0, 6.0, ((0, 16), (2, 2)))
    fwd_mem = scatter_about(arg_keys[1], (N_SECTION, ROWS, D), 1.0, 6.0, ((0, 16), (2, 2)))
    saved_h = scatter_about(arg_keys[2], (N_SECTION, ROWS, D), 1.0, 6.0, ((0, 16), (2, 2)))
    saved_mem = scatter_about(arg_keys[3], (N_SECTION, ROWS, D), 1.0, 6.0, ((0, 16), (2, 2)))
    back_h = scatter_about(arg_keys[4], (N_SECTION, ROWS, D), 1.0, 6.0, ((0, 16), (2, 2)))
    back_mem = scatter_about(arg_keys[5], (N_SECTION, ROWS, D), 1.0, 6.0, ((0, 16), (2, 2)))
    weight = scatter_about(arg_keys[6], (N_SECTION, D, INNER), D ** -0.5, 0.125, ((0, 16), (2, 2)))
    row_stat = jnp.clip(jnp.exp(math.log(5.0) - 4.6051702 * jax.random.uniform(arg_keys[7], (N_SECTION, D), jnp.float32) ** levels(arg_keys[7], (N_SECTION, D), ((0, 16),), -0.2, 0.2)), 0.05, 5.0)
    col_stat = jnp.clip(jnp.exp(math.log(5.0) - 4.6051702 * jax.random.uniform(arg_keys[8], (N_SECTION, INNER), jnp.float32) ** levels(arg_keys[8], (N_SECTION, INNER), ((0, 16), (1, 2)), -0.2, 0.2)), 0.05, 5.0)
    enc_count = jax.random.randint(arg_keys[9], (1,), N_SECTION // 4, 3 * N_SECTION // 4 + 1).astype(jnp.int32)
    target_embed = scatter_about(arg_keys[10], (ROWS, D), 1.0, 6.0, ((1, 2),))
    return dict(fwd_h=fwd_h, fwd_mem=fwd_mem, saved_h=saved_h, saved_mem=saved_mem, back_h=back_h, back_mem=back_mem, weight=weight, row_stat=row_stat, col_stat=col_stat, enc_count=enc_count, target_embed=target_embed)


EPS = 1e-06
BETA = 0.8
TINY = 1e-30

def normalize(values):
    inv = lax.rsqrt(lax.optimization_barrier(jnp.mean(values * values, axis=-1, keepdims=True)) + EPS)
    return (values * inv, inv)

def attend(hn, cn, weight):
    scale = 1.0 / HD ** 0.5
    queries = jnp.dot(hn, weight, preferred_element_type=jnp.float32).astype(jnp.bfloat16)
    keyvals = jnp.dot(cn, weight, preferred_element_type=jnp.float32).astype(jnp.bfloat16)
    q3 = queries.reshape(ROWS, HEADS, HD)
    kv3 = keyvals.reshape(ROWS, HEADS, HD)
    scores = jnp.einsum('qhd,khd->hqk', q3.astype(jnp.float32), kv3.astype(jnp.float32)) * scale
    probs = jax.nn.softmax(scores, axis=-1)
    probs_b = probs.astype(jnp.bfloat16)
    mixed = jnp.einsum('hqk,khd->qhd', probs_b.astype(jnp.float32), kv3.astype(jnp.float32))
    return (q3, kv3, probs, probs_b, mixed.astype(jnp.bfloat16).reshape(ROWS, INNER))

def attend_back(q3, kv3, probs, probs_b, dmix):
    scale = 1.0 / HD ** 0.5
    d3 = dmix.reshape(ROWS, HEADS, HD).astype(jnp.float32)
    kvf = kv3.astype(jnp.float32)
    dprobs = jnp.einsum('qhd,khd->hqk', d3, kvf)
    dval = jnp.einsum('hqk,qhd->khd', probs_b.astype(jnp.float32), d3)
    dscore = (probs * (dprobs - lax.optimization_barrier(jnp.sum(dprobs * probs, axis=-1, keepdims=True))) * scale).astype(jnp.bfloat16)
    dsf = dscore.astype(jnp.float32)
    dq = jnp.einsum('hqk,khd->qhd', dsf, kvf).astype(jnp.bfloat16)
    dk = jnp.einsum('hqk,qhd->khd', dsf, q3.astype(jnp.float32))
    dkv = (dk + dval).astype(jnp.bfloat16)
    return (dq.reshape(ROWS, INNER), dkv.reshape(ROWS, INNER))

def group_sum(left, weight):
    width = INNER // N_DP
    left3 = left.reshape(ROWS, N_DP, width)
    right3 = weight.astype(jnp.float32).reshape(D, N_DP, width)
    parts = jnp.einsum('rgk,dgk->grd', left3, right3)
    return lax.optimization_barrier(jnp.sum(parts.astype(jnp.bfloat16).astype(jnp.float32), axis=0))

def one_section(items, target_embed, first_dec):
    fh, fm, sh, sm, bh, bm, weight, rows, cols, index = items
    decoder = index >= first_dec
    enc_flag = 1.0 - decoder.astype(jnp.float32)
    inputs = jnp.where(index == first_dec, target_embed, fh)
    context = jnp.where(decoder, fm, inputs)
    hn_f, unused_h = normalize(inputs.astype(jnp.float32))
    cn_f, unused_c = normalize(context.astype(jnp.float32))
    parts = attend(hn_f.astype(jnp.bfloat16), cn_f.astype(jnp.bfloat16), weight)
    out = group_sum(parts[4].astype(jnp.float32), weight)
    result = (inputs.astype(jnp.float32) + out).astype(jnp.bfloat16)
    carry_mem = jnp.where(decoder, fm, result)
    grad_in = jnp.where(index == first_dec - 1, bm, bh)
    old_ctx = jnp.where(decoder, sm, sh)
    hn2_f, inv_h = normalize(sh.astype(jnp.float32))
    cn2_f, inv_c = normalize(old_ctx.astype(jnp.float32))
    hn2 = hn2_f.astype(jnp.bfloat16)
    cn2 = cn2_f.astype(jnp.bfloat16)
    q3, kv3, probs, probs_b, mixed = attend(hn2, cn2, weight)
    dmix = jnp.dot(grad_in, weight, preferred_element_type=jnp.float32).astype(jnp.bfloat16)
    dq, dkv = attend_back(q3, kv3, probs, probs_b, dmix)
    grad_w = jnp.dot(hn2.T, dq, preferred_element_type=jnp.float32)
    grad_w = grad_w + jnp.dot(cn2.T, dkv, preferred_element_type=jnp.float32)
    grad_w = grad_w + jnp.dot(grad_in.T, mixed, preferred_element_type=jnp.float32)
    dqf = dq.astype(jnp.float32)
    dkvf = dkv.astype(jnp.float32)
    width = INNER // N_DP
    wf = weight.astype(jnp.float32).reshape(D, N_DP, width)
    back_q = jnp.einsum('rgk,dgk->grd', dqf.reshape(ROWS, N_DP, width), wf)
    back_kv = jnp.einsum('rgk,dgk->grd', dkvf.reshape(ROWS, N_DP, width), wf)
    dhn = lax.optimization_barrier(jnp.sum((back_q + enc_flag * back_kv).astype(jnp.bfloat16).astype(jnp.float32), axis=0))
    dcn = lax.optimization_barrier(jnp.sum(((1.0 - enc_flag) * back_kv).astype(jnp.bfloat16).astype(jnp.float32), axis=0))
    grad_h = inv_h * (dhn - hn2_f * lax.optimization_barrier(jnp.mean(dhn * hn2_f, axis=-1, keepdims=True)))
    grad_c = inv_c * (dcn - cn2_f * lax.optimization_barrier(jnp.mean(dcn * cn2_f, axis=-1, keepdims=True)))
    send_h = (grad_in.astype(jnp.float32) + grad_h).astype(jnp.bfloat16)
    send_mem = jnp.where(decoder, bm.astype(jnp.float32) + grad_c, 0.0).astype(jnp.bfloat16)
    squares = grad_w * grad_w
    row_next = BETA * rows + (1.0 - BETA) * (lax.optimization_barrier(jnp.mean(squares, axis=1)) + TINY)
    col_next = BETA * cols + (1.0 - BETA) * (lax.optimization_barrier(jnp.mean(squares, axis=0)) + TINY)
    step = grad_w * lax.rsqrt(row_next[:, None] * col_next[None, :] / jnp.mean(row_next))
    root = jnp.sqrt(jnp.mean(step * step))
    update = (step / jnp.maximum(1.0, root)).astype(jnp.bfloat16)
    return (result, carry_mem, send_h, send_mem, update, row_next, col_next)

def reference(fwd_h, fwd_mem, saved_h, saved_mem, back_h, back_mem, weight, row_stat, col_stat, enc_count, target_embed):
    first_dec = enc_count[0]
    index = jnp.arange(N_SECTION, dtype=jnp.int32)
    items = (fwd_h, fwd_mem, saved_h, saved_mem, back_h, back_mem, weight, row_stat, col_stat, index)
    result, carry_mem, send_h, send_mem, update, row_next, col_next = lax.map(lambda item: one_section(item, target_embed, first_dec), items)
    blank = jnp.zeros((1, ROWS, D), jnp.bfloat16)
    next_h = jnp.concatenate([blank, result[:-1]], axis=0)
    next_mem = jnp.concatenate([blank, carry_mem[:-1]], axis=0)
    prev_h = jnp.concatenate([send_h[1:], blank], axis=0)
    prev_mem = jnp.concatenate([send_mem[1:], blank], axis=0)
    return (next_h, next_mem, prev_h, prev_mem, update, row_next, col_next)
```

```python
import functools

import jax
import jax.numpy as jnp
from jax import lax
from jax.experimental import pallas as pl
from jax.experimental.pallas import tpu as pltpu
from jax.sharding import PartitionSpec as P

HD = 256
EPS = 1e-06
BETA = 0.8
TINY = 1e-30
SCALE = 1.0 / HD**0.5
MESH = pl.DeviceIdType.MESH
F32 = jnp.float32
BF16 = jnp.bfloat16
MIB = 1024 * 1024


def dot_nn(a, b):
    return lax.dot_general(a, b, (((1,), (0,)), ((), ())), preferred_element_type=F32)


def dot_nt(a, b):
    return lax.dot_general(a, b, (((1,), (1,)), ((), ())), preferred_element_type=F32)


def dot_tn(a, b):
    return lax.dot_general(a, b, (((0,), (0,)), ((), ())), preferred_element_type=F32)


def lanes_to_rows(first, second):
    rows = first.shape[0]
    lane = lax.broadcasted_iota(jnp.int32, (rows, 128), 1)
    both = jnp.where(lane == 0, first, second)
    return jnp.transpose(both)[0:8]


def rows_to_lanes(row):
    return jnp.transpose(jnp.broadcast_to(row, (128, row.shape[1])))


def kernel(
    n, sections, rows, width, cols, tile,
    fwd_h, fwd_mem, saved_h, saved_mem, back_h, back_mem, weight, row_stat, col_stat, count, target,
    next_h, got_mem, prev_h, prev_mem, update, row_new, col_new,
    proj, sh, sm, xh, xm, tmp, left, fleft, qkv, probs, right, fmix,
    th, tc, out, th_in, tc_in, out_in, inv, stats, grad, sums, acc, upd, send_h, send_m, send_y,
    local_sem, gather_s, gather_r, part_s, part_r, small_s, small_r, sec_s, sec_r,
):
    me = lax.axis_index("dp")
    s = lax.axis_index("section")
    tiles = width // tile
    heads = cols // HD
    full = n * width
    r2, r3 = 2 * rows, 3 * rows
    first_dec = count[0]
    dec = (s >= first_dec).astype(jnp.int32)
    is_first = (s == first_dec).astype(jnp.int32)
    is_last_enc = (s == first_dec - 1).astype(jnp.int32)
    own_tmp = [tmp.at[i] for i in range(4)]

    def peer(k):
        return lax.rem(me + k, n)

    def source(k):
        return lax.rem(me + n - k, n)

    loads = [
        (back_h.at[0], own_tmp[0]),
        (back_mem.at[0], own_tmp[1]),
        (fwd_h.at[0], own_tmp[2]),
        (target, own_tmp[3]),
        (saved_h.at[0], sh.at[me]),
        (saved_mem.at[0], sm.at[me]),
        (weight.at[0], proj),
        (fwd_mem.at[0], xm.at[me]),
    ]
    loads = [pltpu.make_async_copy(a, b, local_sem.at[i]) for i, (a, b) in enumerate(loads)]
    for load in loads:
        load.start()

    barrier = pltpu.get_barrier_semaphore()
    for k in range(1, n):
        pl.semaphore_signal(barrier, 1, device_id={"dp": peer(k)}, device_id_type=MESH)

    @pl.when(s > 0)
    def _():
        pl.semaphore_signal(barrier, 1, device_id={"section": s - 1}, device_id_type=MESH)

    @pl.when(s < sections - 1)
    def _():
        pl.semaphore_signal(barrier, 1, device_id={"section": s + 1}, device_id_type=MESH)

    ends = (s > 0).astype(jnp.int32) + (s < sections - 1).astype(jnp.int32)
    pl.semaphore_wait(barrier, n - 1 + ends)

    def to_peer(src, dst, send, recv, k):
        return pltpu.make_async_remote_copy(
            src, dst, send, recv, device_id={"dp": peer(k)}, device_id_type=MESH
        )

    def gather_start(i, src, slot):
        for k in range(1, n):
            to_peer(src, slot(me), gather_s.at[i, k - 1], gather_r.at[i, k - 1], k).start()

    def gather_wait(i, src, slot):
        for k in range(1, n):
            to_peer(src, slot(me), gather_s.at[i, k - 1], gather_r.at[i, k - 1], k).wait_send()
            got = slot(source(k))
            to_peer(got, got, gather_s.at[i, k - 1], gather_r.at[i, k - 1], k).wait_recv()

    def g_slot(p):
        return left.at[p, pl.ds(r2, rows)]

    gather_start(0, saved_h.at[0], lambda p: sh.at[p])
    gather_start(1, saved_mem.at[0], lambda p: sm.at[p])

    def section_copy(i, t, src, dst, by):
        return pltpu.make_async_remote_copy(
            src, dst, sec_s.at[i, t], sec_r.at[i, t],
            device_id={"section": s + by}, device_id_type=MESH,
        )

    @pl.when(s < sections - 1)
    def _():
        section_copy(0, 0, fwd_mem.at[0], got_mem.at[0], 1).start()

    def select(flag, yes, no, dst):
        step = 32

        def body(i, carry):
            at = pl.ds(pl.multiple_of(i * step, step), step)
            mask = jnp.full((step, width), flag, jnp.int32) > 0
            dst[at, :] = jnp.where(mask, yes[at, :].astype(F32), no[at, :].astype(F32)).astype(BF16)
            return carry

        lax.fori_loop(0, rows // step, body, 0)

    for i in range(4):
        loads[i].wait()
    select(is_last_enc, own_tmp[1], own_tmp[0], left.at[me, pl.ds(r2, rows)])
    select(is_first, own_tmp[3], own_tmp[2], xh.at[me])

    def normalize(h_ref, m_ref, dst, keep):
        step = 32

        def body(i, carry):
            at = pl.ds(pl.multiple_of(i * step, step), step)
            at_c = pl.ds(pl.multiple_of(rows + i * step, step), step)
            h = [h_ref[p, at, :].astype(F32) for p in range(n)]
            mask = jnp.full((step, width), dec, jnp.int32) > 0
            c = [jnp.where(mask, m_ref[p, at, :].astype(F32), h[p]) for p in range(n)]
            for j, (v, where) in enumerate(((h, at), (c, at_c))):
                total = sum(jnp.sum(x * x, axis=1, keepdims=True) for x in v)
                r = lax.rsqrt(total / full + EPS)
                for p in range(n):
                    dst[p, where, :] = (v[p] * r).astype(BF16)
                if keep:
                    inv[j, at, :] = jnp.broadcast_to(r, (step, 128))
            return carry

        lax.fori_loop(0, rows // step, body, 0)

    def head_cols(h):
        return pl.ds(pl.multiple_of(h * HD, HD), HD)

    def project(src, lo, size, at):
        return sum(
            dot_nn(src[p, lo : lo + size, :], proj[p * width : (p + 1) * width, at])
            for p in range(n)
        )

    def softmax(q, kv):
        score = dot_nt(q, kv) * SCALE
        e = jnp.exp(score - jnp.max(score, axis=1, keepdims=True))
        return e / jnp.sum(e, axis=1, keepdims=True)

    loads[4].wait()
    loads[5].wait()
    gather_wait(0, saved_h.at[0], lambda p: sh.at[p])
    gather_start(2, g_slot(me), g_slot)
    gather_wait(1, saved_mem.at[0], lambda p: sm.at[p])
    gather_start(3, xh.at[me], lambda p: xh.at[p])
    normalize(sh, sm, left, True)
    loads[6].wait()

    def attend_body(h, carry):
        at = head_cols(h)
        both = project(left, 0, r2, at).astype(BF16)
        qkv[:, at] = both
        q, kv = both[:rows], both[rows:]
        p = softmax(q, kv)
        probs[h] = p
        right[r2:r3, at] = dot_nn(p.astype(BF16), kv).astype(BF16)
        return carry

    lax.fori_loop(0, heads, attend_body, 0)

    gather_wait(2, g_slot(me), g_slot)
    gather_start(4, fwd_mem.at[0], lambda p: xm.at[p])

    def back_body(h, carry):
        stat_q, stat_k = carry
        at = head_cols(h)
        dmix = project(left, r2, rows, at).astype(BF16)
        q, kv = qkv[0:rows, at], qkv[rows:r2, at]
        p = probs[h]
        dprobs = dot_nt(dmix, kv)
        dval = dot_tn(p.astype(BF16), dmix)
        inner = jnp.sum(dprobs * p, axis=1, keepdims=True)
        dscore = (p * (dprobs - inner) * SCALE).astype(BF16)
        dq = dot_nn(dscore, kv).astype(BF16)
        dkv = (dot_tn(dscore, q) + dval).astype(BF16)
        right[0:rows, at] = dq
        right[rows:r2, at] = dkv
        stat_q += jnp.sum(dq.astype(F32) * q.astype(F32), axis=1, keepdims=True)
        stat_k += jnp.sum(dkv.astype(F32) * kv.astype(F32), axis=1, keepdims=True)
        return stat_q, stat_k

    zero_col = jnp.zeros((rows, 1), F32)
    stat_q, stat_k = lax.fori_loop(0, heads, back_body, (zero_col, zero_col))
    decf = jnp.full((rows, 1), dec, jnp.int32).astype(F32)
    stats[me] = lanes_to_rows(stat_q + (1.0 - decf) * stat_k, decf * stat_k)
    for k in range(1, n):
        to_peer(stats.at[me], stats.at[me], small_s.at[0, k - 1], small_r.at[0, k - 1], k).start()

    def row_tile(p, t):
        return pl.ds(pl.multiple_of(p * width + t * tile, tile), tile)

    def terms(p, t, to_h, to_c):
        both = dot_nt(right[0:r2, :], proj[row_tile(p, t), :])
        bq, bk = both[:rows], both[rows:]
        flag = jnp.full((rows, tile), dec, jnp.int32).astype(F32)
        to_h[...] = (bq + (1.0 - flag) * bk).astype(BF16)
        to_c[...] = (flag * bk).astype(BF16)

    def part_copy(i, k, t, src, dst):
        return to_peer(
            src.at[k - 1, t], dst.at[k, t], part_s.at[i, k - 1, t], part_r.at[i, k - 1, t], k
        )

    for k in range(1, n):
        for t in range(tiles):
            terms(peer(k), t, th.at[k - 1, t], tc.at[k - 1, t])
            part_copy(0, k, t, th, th_in).start()
            part_copy(1, k, t, tc, tc_in).start()

    def own_terms(t, carry):
        terms(me, t, th_in.at[0, t], tc_in.at[0, t])
        return carry

    lax.fori_loop(0, tiles, own_terms, 0)

    loads[7].wait()
    gather_wait(3, xh.at[me], lambda p: xh.at[p])
    gather_wait(4, fwd_mem.at[0], lambda p: xm.at[p])
    normalize(xh, xm, fleft, False)

    def forward_body(h, carry):
        at = head_cols(h)
        both = project(fleft, 0, r2, at).astype(BF16)
        kv = both[rows:]
        p = softmax(both[:rows], kv).astype(BF16)
        fmix[:, at] = dot_nn(p, kv).astype(BF16)
        return carry

    lax.fori_loop(0, heads, forward_body, 0)
    for k in range(1, n):
        for t in range(tiles):
            out[k - 1, t] = dot_nt(fmix[...], proj[row_tile(peer(k), t), :]).astype(BF16)
            part_copy(2, k, t, out, out_in).start()

    def own_out(t, carry):
        out_in[0, t] = dot_nt(fmix[...], proj[row_tile(me, t), :]).astype(BF16)
        return carry

    lax.fori_loop(0, tiles, own_out, 0)

    acc[...] = jnp.zeros_like(acc)

    def grad_body(f, carry):
        p, t = f // tiles, f % tiles
        tl = left[p, :, pl.ds(pl.multiple_of(t * tile, tile), tile)]
        g = dot_tn(tl, right[...])
        grad[pl.ds(pl.multiple_of(f * tile, tile), tile), :] = g
        acc[...] += jnp.sum((g * g).reshape(tile // 8, 8, cols), axis=0)
        return carry

    lax.fori_loop(0, n * tiles, grad_body, 0)
    col = BETA * col_stat[...] + (1.0 - BETA) * (
        jnp.sum(acc[...], axis=0, keepdims=True) / full + TINY
    )
    col_new[...] = col
    inv_col = 1.0 / col

    step = 128

    def sums_body(i, carry):
        at = pl.ds(pl.multiple_of(i * step, step), step)
        g = grad[at, :]
        g = g * g
        sums[me, :, at] = lanes_to_rows(
            jnp.sum(g, axis=1, keepdims=True), jnp.sum(g * inv_col, axis=1, keepdims=True)
        )
        return carry

    lax.fori_loop(0, full // step, sums_body, 0)
    for k in range(1, n):
        to_peer(sums.at[me], sums.at[me], small_s.at[1, k - 1], small_r.at[1, k - 1], k).start()

    def small_wait(i, ref):
        for k in range(1, n):
            to_peer(
                ref.at[me], ref.at[me], small_s.at[i, k - 1], small_r.at[i, k - 1], k
            ).wait_send()
            got = ref.at[source(k)]
            to_peer(got, got, small_s.at[i, k - 1], small_r.at[i, k - 1], k).wait_recv()

    small_wait(0, stats)
    stat = sum(stats[p] for p in range(n)) / full
    stat_h, stat_c = rows_to_lanes(stat[0:1])[:, 0:1], rows_to_lanes(stat[1:2])[:, 0:1]

    def tile_cols(t):
        return slice(t * tile, (t + 1) * tile)

    for t in range(tiles):
        for k in range(1, n):
            part_copy(0, k, t, th, th_in).wait()
            part_copy(1, k, t, tc, tc_in).wait()
        share_h = sum(th_in[k, t].astype(F32) for k in range(n))
        share_c = sum(tc_in[k, t].astype(F32) for k in range(n))
        at = tile_cols(t)
        inv_h, inv_c = inv[0][:, 0:1], inv[1][:, 0:1]
        grad_h = inv_h * (share_h - sh[me, :, at].astype(F32) * inv_h * stat_h)
        grad_c = inv_c * (share_c - sm[me, :, at].astype(F32) * inv_c * stat_c)
        send_h[t] = (left[me, r2:r3, at].astype(F32) + grad_h).astype(BF16)
        mask = jnp.full((rows, tile), dec, jnp.int32) > 0
        send_m[t] = jnp.where(mask, own_tmp[1][:, at].astype(F32) + grad_c, 0.0).astype(BF16)

        @pl.when(s > 0)
        def _():
            section_copy(1, t, send_h.at[t], prev_h.at[0, :, pl.ds(t * tile, tile)], -1).start()
            section_copy(2, t, send_m.at[t], prev_mem.at[0, :, pl.ds(t * tile, tile)], -1).start()

    for t in range(tiles):
        for k in range(1, n):
            part_copy(2, k, t, out, out_in).wait()
        at = tile_cols(t)
        share = sum(out_in[k, t].astype(F32) for k in range(n))
        send_y[t] = (xh[me, :, at].astype(F32) + share).astype(BF16)

        @pl.when(s < sections - 1)
        def _():
            section_copy(3, t, send_y.at[t], next_h.at[0, :, pl.ds(t * tile, tile)], 1).start()

    small_wait(1, sums)
    total = sum(sums[p] for p in range(n))
    row = BETA * row_stat[...] + (1.0 - BETA) * (total[0:1] / (n * cols) + TINY)
    row_new[...] = row
    mean_row = jnp.sum(row, axis=1, keepdims=True) / full
    total_sq = mean_row * jnp.sum(total[1:2] / row, axis=1, keepdims=True)
    root = jnp.sqrt(total_sq / (full * (n * cols)))
    sums[me, 0:1, :] = lax.rsqrt(row) * (jnp.sqrt(mean_row) / jnp.maximum(1.0, root))
    root_col = lax.rsqrt(col)

    def update_copy(at, i):
        return pltpu.make_async_copy(upd.at[at], update.at[0, at], local_sem.at[i])

    def update_body(i, carry):
        at = pl.ds(pl.multiple_of(i * step, step), step)
        factor = rows_to_lanes(sums[me, 0:1, at])[:, 0:1]
        upd[at, :] = (grad[at, :] * factor * root_col).astype(BF16)
        return carry

    pieces = 4
    size = full // pieces
    for j in range(pieces):
        lax.fori_loop(j * (size // step), (j + 1) * (size // step), update_body, 0)
        update_copy(pl.ds(j * size, size), 8 + j).start()

    @pl.when(s == 0)
    def _():
        own_tmp[0][...] = jnp.zeros((rows, width), BF16)
        for i, dst in enumerate((next_h, got_mem)):
            pltpu.make_async_copy(own_tmp[0], dst.at[0], local_sem.at[i]).start()
        for i, dst in enumerate((next_h, got_mem)):
            pltpu.make_async_copy(own_tmp[0], dst.at[0], local_sem.at[i]).wait()

    @pl.when(s == sections - 1)
    def _():
        own_tmp[0][...] = jnp.zeros((rows, width), BF16)
        for i, dst in enumerate((prev_h, prev_mem)):
            pltpu.make_async_copy(own_tmp[0], dst.at[0], local_sem.at[i]).start()
        for i, dst in enumerate((prev_h, prev_mem)):
            pltpu.make_async_copy(own_tmp[0], dst.at[0], local_sem.at[i]).wait()

    @pl.when(s < sections - 1)
    def _():
        section_copy(0, 0, fwd_mem.at[0], got_mem.at[0], 1).wait_send()
        for t in range(tiles):
            at = pl.ds(t * tile, tile)
            section_copy(3, t, send_y.at[t], next_h.at[0, :, at], 1).wait_send()
            section_copy(1, t, send_h.at[t], prev_h.at[0, :, at], 1).wait_recv()
            section_copy(2, t, send_m.at[t], prev_mem.at[0, :, at], 1).wait_recv()

    @pl.when(s > 0)
    def _():
        section_copy(0, 0, fwd_mem.at[0], got_mem.at[0], -1).wait_recv()
        for t in range(tiles):
            at = pl.ds(t * tile, tile)
            section_copy(3, t, send_y.at[t], next_h.at[0, :, at], -1).wait_recv()
            section_copy(1, t, send_h.at[t], prev_h.at[0, :, at], -1).wait_send()
            section_copy(2, t, send_m.at[t], prev_mem.at[0, :, at], -1).wait_send()

    for j in range(pieces):
        update_copy(pl.ds(j * size, size), 8 + j).wait()


def on_device(
    n, sections,
    fwd_h, fwd_mem, saved_h, saved_mem, back_h, back_mem, weight, row_stat, col_stat, enc_count,
    target_embed,
):
    rows, width = fwd_h.shape[1:]
    cols = weight.shape[2]
    full = n * width
    tile = min(256, width)
    tiles = width // tile
    heads = cols // HD
    hbm = pl.BlockSpec(memory_space=pl.ANY)
    vmem = pl.BlockSpec(memory_space=pltpu.VMEM)
    smem = pl.BlockSpec(memory_space=pltpu.SMEM)
    act = jax.ShapeDtypeStruct((1, rows, width), BF16)
    dma = pltpu.SemaphoreType.DMA
    parts = pltpu.VMEM((n, tiles, rows, tile), BF16)
    others = pltpu.VMEM((n - 1, tiles, rows, tile), BF16)
    stored = pltpu.VMEM((n, rows, width), BF16)
    result = pltpu.VMEM((tiles, rows, tile), BF16)
    next_h, got_mem, prev_h, prev_mem, update, row_new, col_new = pl.pallas_call(
        functools.partial(kernel, n, sections, rows, width, cols, tile),
        out_shape=(
            act, act, act, act,
            jax.ShapeDtypeStruct((1, full, cols), BF16),
            jax.ShapeDtypeStruct((1, full), F32),
            jax.ShapeDtypeStruct((1, cols), F32),
        ),
        in_specs=[hbm] * 7 + [vmem, vmem, smem, hbm],
        out_specs=[hbm] * 5 + [vmem, vmem],
        scratch_shapes=[
            pltpu.VMEM((full, cols), BF16),
            stored, stored, stored, stored,
            pltpu.VMEM((4, rows, width), BF16),
            pltpu.VMEM((n, 3 * rows, width), BF16),
            pltpu.VMEM((n, 2 * rows, width), BF16),
            pltpu.VMEM((2 * rows, cols), BF16),
            pltpu.VMEM((heads, rows, rows), F32),
            pltpu.VMEM((3 * rows, cols), BF16),
            pltpu.VMEM((rows, cols), BF16),
            others, others, others, parts, parts, parts,
            pltpu.VMEM((2, rows, 128), F32),
            pltpu.VMEM((n, 8, rows), F32),
            pltpu.VMEM((full, cols), F32),
            pltpu.VMEM((n, 8, full), F32),
            pltpu.VMEM((8, cols), F32),
            pltpu.VMEM((full, cols), BF16),
            result, result, result,
            dma((12,)),
            dma((5, n - 1)), dma((5, n - 1)),
            dma((3, n - 1, tiles)), dma((3, n - 1, tiles)),
            dma((2, n - 1)), dma((2, n - 1)),
            dma((4, tiles)), dma((4, tiles)),
        ],
        compiler_params=pltpu.CompilerParams(
            collective_id=0, has_side_effects=True, vmem_limit_bytes=58 * MIB
        ),
    )(
        fwd_h, fwd_mem, saved_h, saved_mem, back_h, back_mem, weight, row_stat, col_stat,
        enc_count, target_embed,
    )
    before_dec = lax.axis_index("section") - 1 >= enc_count[0]
    next_mem = jnp.where(before_dec, got_mem, next_h)
    return (next_h, next_mem, prev_h, prev_mem, update, row_new, col_new)


def solution(mesh):
    act = P("section", None, "dp")
    in_specs = (
        act, act, act, act, act, act, act, P("section", None), P("section", "dp"), P(), P(None, "dp"),
    )
    out_specs = (act, act, act, act, act, P("section", None), P("section", "dp"))
    body = functools.partial(on_device, mesh.shape["dp"], mesh.shape["section"])
    return jax.shard_map(
        body, mesh=mesh, in_specs=in_specs, out_specs=out_specs, check_vma=False
    )
```

```python
import functools

import jax
import jax.numpy as jnp
from jax import lax
from jax.experimental import pallas as pl
from jax.experimental.pallas import tpu as pltpu
from jax.sharding import PartitionSpec as P

HD = 256
EPS = 1e-06
BETA = 0.8
TINY = 1e-30
SCALE = 1.0 / HD**0.5
MESH = pl.DeviceIdType.MESH
F32 = jnp.float32
BF16 = jnp.bfloat16
MIB = 1024 * 1024


def dot_nn(a, b):
    return lax.dot_general(a, b, (((1,), (0,)), ((), ())), preferred_element_type=F32)


def dot_nt(a, b):
    return lax.dot_general(a, b, (((1,), (1,)), ((), ())), preferred_element_type=F32)


def dot_tn(a, b):
    return lax.dot_general(a, b, (((0,), (0,)), ((), ())), preferred_element_type=F32)


def lanes_to_rows(first, second):
    rows = first.shape[0]
    lane = lax.broadcasted_iota(jnp.int32, (rows, 128), 1)
    both = jnp.where(lane == 0, first, second)
    return jnp.transpose(both)[0:8]


def rows_to_lanes(row):
    return jnp.transpose(jnp.broadcast_to(row, (128, row.shape[1])))


def kernel(
    n, sections, rows, width, cols, tile,
    fwd_h, fwd_mem, saved_h, saved_mem, back_h, back_mem, weight, row_stat, col_stat, count, target,
    next_h, got_mem, prev_h, prev_mem, update, row_new, col_new,
    proj, sh, sm, xh, xm, tmp, left, fleft, qkv, probs, right, fmix,
    th, tc, out, th_in, tc_in, out_in, inv, stats, grad, sums, acc, send_h, send_m, send_y,
    local_sem, gather_s, gather_r, part_s, part_r, small_s, small_r, sec_s, sec_r,
):
    me = lax.axis_index("dp")
    s = lax.axis_index("section")
    tiles = width // tile
    heads = cols // HD
    full = n * width
    r2, r3 = 2 * rows, 3 * rows
    first_dec = count[0]
    dec = (s >= first_dec).astype(jnp.int32)
    is_first = (s == first_dec).astype(jnp.int32)
    is_last_enc = (s == first_dec - 1).astype(jnp.int32)
    own_tmp = [tmp.at[i] for i in range(4)]

    def peer(k):
        return lax.rem(me + k, n)

    def source(k):
        return lax.rem(me + n - k, n)

    loads = [
        (back_h.at[0], own_tmp[0]),
        (back_mem.at[0], own_tmp[1]),
        (fwd_h.at[0], own_tmp[2]),
        (target, own_tmp[3]),
        (saved_h.at[0], sh.at[me]),
        (saved_mem.at[0], sm.at[me]),
        (weight.at[0], proj),
        (fwd_mem.at[0], xm.at[me]),
    ]
    loads = [pltpu.make_async_copy(a, b, local_sem.at[i]) for i, (a, b) in enumerate(loads)]
    for load in loads:
        load.start()

    barrier = pltpu.get_barrier_semaphore()
    for k in range(1, n):
        pl.semaphore_signal(barrier, 1, device_id={"dp": peer(k)}, device_id_type=MESH)

    @pl.when(s > 0)
    def _():
        pl.semaphore_signal(barrier, 1, device_id={"section": s - 1}, device_id_type=MESH)

    @pl.when(s < sections - 1)
    def _():
        pl.semaphore_signal(barrier, 1, device_id={"section": s + 1}, device_id_type=MESH)

    ends = (s > 0).astype(jnp.int32) + (s < sections - 1).astype(jnp.int32)
    pl.semaphore_wait(barrier, n - 1 + ends)

    def to_peer(src, dst, send, recv, k):
        return pltpu.make_async_remote_copy(
            src, dst, send, recv, device_id={"dp": peer(k)}, device_id_type=MESH
        )

    def gather_start(i, src, slot):
        for k in range(1, n):
            to_peer(src, slot(me), gather_s.at[i, k - 1], gather_r.at[i, k - 1], k).start()

    def gather_wait(i, src, slot):
        for k in range(1, n):
            to_peer(src, slot(me), gather_s.at[i, k - 1], gather_r.at[i, k - 1], k).wait_send()
            got = slot(source(k))
            to_peer(got, got, gather_s.at[i, k - 1], gather_r.at[i, k - 1], k).wait_recv()

    def g_slot(p):
        return left.at[p, pl.ds(r2, rows)]

    gather_start(0, saved_h.at[0], lambda p: sh.at[p])
    gather_start(1, saved_mem.at[0], lambda p: sm.at[p])

    def section_copy(i, t, src, dst, by):
        return pltpu.make_async_remote_copy(
            src, dst, sec_s.at[i, t], sec_r.at[i, t],
            device_id={"section": s + by}, device_id_type=MESH,
        )

    @pl.when(s < sections - 1)
    def _():
        section_copy(0, 0, fwd_mem.at[0], got_mem.at[0], 1).start()

    def select(flag, yes, no, dst):
        step = 32

        def body(i, carry):
            at = pl.ds(pl.multiple_of(i * step, step), step)
            mask = jnp.full((step, width), flag, jnp.int32) > 0
            dst[at, :] = jnp.where(mask, yes[at, :].astype(F32), no[at, :].astype(F32)).astype(BF16)
            return carry

        lax.fori_loop(0, rows // step, body, 0)

    for i in range(4):
        loads[i].wait()
    select(is_last_enc, own_tmp[1], own_tmp[0], left.at[me, pl.ds(r2, rows)])
    select(is_first, own_tmp[3], own_tmp[2], xh.at[me])

    def normalize(h_ref, m_ref, dst, keep):
        step = 32

        def body(i, carry):
            at = pl.ds(pl.multiple_of(i * step, step), step)
            at_c = pl.ds(pl.multiple_of(rows + i * step, step), step)
            h = [h_ref[p, at, :].astype(F32) for p in range(n)]
            mask = jnp.full((step, width), dec, jnp.int32) > 0
            c = [jnp.where(mask, m_ref[p, at, :].astype(F32), h[p]) for p in range(n)]
            for j, (v, where) in enumerate(((h, at), (c, at_c))):
                total = sum(jnp.sum(x * x, axis=1, keepdims=True) for x in v)
                r = lax.rsqrt(total / full + EPS)
                for p in range(n):
                    dst[p, where, :] = (v[p] * r).astype(BF16)
                if keep:
                    inv[j, at, :] = jnp.broadcast_to(r, (step, 128))
            return carry

        lax.fori_loop(0, rows // step, body, 0)

    def head_cols(h):
        return pl.ds(pl.multiple_of(h * HD, HD), HD)

    def project(src, lo, size, at):
        return sum(
            dot_nn(src[p, lo : lo + size, :], proj[p * width : (p + 1) * width, at])
            for p in range(n)
        )

    def softmax(q, kv):
        score = dot_nt(q, kv) * SCALE
        e = jnp.exp(score - jnp.max(score, axis=1, keepdims=True))
        return e / jnp.sum(e, axis=1, keepdims=True)

    loads[4].wait()
    loads[5].wait()
    gather_wait(0, saved_h.at[0], lambda p: sh.at[p])
    gather_start(2, g_slot(me), g_slot)
    gather_wait(1, saved_mem.at[0], lambda p: sm.at[p])
    gather_start(3, xh.at[me], lambda p: xh.at[p])
    normalize(sh, sm, left, True)
    loads[6].wait()

    def attend_body(h, carry):
        at = head_cols(h)
        both = project(left, 0, r2, at).astype(BF16)
        qkv[:, at] = both
        q, kv = both[:rows], both[rows:]
        p = softmax(q, kv)
        probs[h] = p
        right[r2:r3, at] = dot_nn(p.astype(BF16), kv).astype(BF16)
        return carry

    lax.fori_loop(0, heads, attend_body, 0)

    gather_wait(2, g_slot(me), g_slot)
    gather_start(4, fwd_mem.at[0], lambda p: xm.at[p])

    def back_body(h, carry):
        stat_q, stat_k = carry
        at = head_cols(h)
        dmix = project(left, r2, rows, at).astype(BF16)
        q, kv = qkv[0:rows, at], qkv[rows:r2, at]
        p = probs[h]
        dprobs = dot_nt(dmix, kv)
        dval = dot_tn(p.astype(BF16), dmix)
        inner = jnp.sum(dprobs * p, axis=1, keepdims=True)
        dscore = (p * (dprobs - inner) * SCALE).astype(BF16)
        dq = dot_nn(dscore, kv).astype(BF16)
        dkv = (dot_tn(dscore, q) + dval).astype(BF16)
        right[0:rows, at] = dq
        right[rows:r2, at] = dkv
        stat_q += jnp.sum(dq.astype(F32) * q.astype(F32), axis=1, keepdims=True)
        stat_k += jnp.sum(dkv.astype(F32) * kv.astype(F32), axis=1, keepdims=True)
        return stat_q, stat_k

    zero_col = jnp.zeros((rows, 1), F32)
    stat_q, stat_k = lax.fori_loop(0, heads, back_body, (zero_col, zero_col))
    decf = jnp.full((rows, 1), dec, jnp.int32).astype(F32)
    stats[me] = lanes_to_rows(stat_q + (1.0 - decf) * stat_k, decf * stat_k)
    for k in range(1, n):
        to_peer(stats.at[me], stats.at[me], small_s.at[0, k - 1], small_r.at[0, k - 1], k).start()

    def row_tile(p, t):
        return pl.ds(pl.multiple_of(p * width + t * tile, tile), tile)

    def terms(p, t, to_h, to_c):
        both = dot_nt(right[0:r2, :], proj[row_tile(p, t), :])
        bq, bk = both[:rows], both[rows:]
        flag = jnp.full((rows, tile), dec, jnp.int32).astype(F32)
        to_h[...] = (bq + (1.0 - flag) * bk).astype(BF16)
        to_c[...] = (flag * bk).astype(BF16)

    def part_copy(i, k, t, src, dst):
        return to_peer(
            src.at[k - 1, t], dst.at[k, t], part_s.at[i, k - 1, t], part_r.at[i, k - 1, t], k
        )

    for k in range(1, n):
        for t in range(tiles):
            terms(peer(k), t, th.at[k - 1, t], tc.at[k - 1, t])
            part_copy(0, k, t, th, th_in).start()
            part_copy(1, k, t, tc, tc_in).start()

    def own_terms(t, carry):
        terms(me, t, th_in.at[0, t], tc_in.at[0, t])
        return carry

    lax.fori_loop(0, tiles, own_terms, 0)

    loads[7].wait()
    gather_wait(3, xh.at[me], lambda p: xh.at[p])
    gather_wait(4, fwd_mem.at[0], lambda p: xm.at[p])
    normalize(xh, xm, fleft, False)

    def forward_body(h, carry):
        at = head_cols(h)
        both = project(fleft, 0, r2, at).astype(BF16)
        kv = both[rows:]
        p = softmax(both[:rows], kv).astype(BF16)
        fmix[:, at] = dot_nn(p, kv).astype(BF16)
        return carry

    lax.fori_loop(0, heads, forward_body, 0)
    for k in range(1, n):
        for t in range(tiles):
            out[k - 1, t] = dot_nt(fmix[...], proj[row_tile(peer(k), t), :]).astype(BF16)
            part_copy(2, k, t, out, out_in).start()

    def own_out(t, carry):
        out_in[0, t] = dot_nt(fmix[...], proj[row_tile(me, t), :]).astype(BF16)
        return carry

    lax.fori_loop(0, tiles, own_out, 0)

    acc[...] = jnp.zeros_like(acc)

    def grad_body(f, carry):
        p, t = f // tiles, f % tiles
        tl = left[p, :, pl.ds(pl.multiple_of(t * tile, tile), tile)]
        g = dot_tn(tl, right[...])
        grad[pl.ds(pl.multiple_of(f * tile, tile), tile), :] = g
        acc[...] += jnp.sum((g * g).reshape(tile // 8, 8, cols), axis=0)
        return carry

    lax.fori_loop(0, n * tiles, grad_body, 0)
    col = BETA * col_stat[...] + (1.0 - BETA) * (
        jnp.sum(acc[...], axis=0, keepdims=True) / full + TINY
    )
    col_new[...] = col
    inv_col = 1.0 / col

    step = 128

    def sums_body(i, carry):
        at = pl.ds(pl.multiple_of(i * step, step), step)
        g = grad[at, :]
        g = g * g
        sums[me, :, at] = lanes_to_rows(
            jnp.sum(g, axis=1, keepdims=True), jnp.sum(g * inv_col, axis=1, keepdims=True)
        )
        return carry

    lax.fori_loop(0, full // step, sums_body, 0)
    for k in range(1, n):
        to_peer(sums.at[me], sums.at[me], small_s.at[1, k - 1], small_r.at[1, k - 1], k).start()

    def small_wait(i, ref):
        for k in range(1, n):
            to_peer(
                ref.at[me], ref.at[me], small_s.at[i, k - 1], small_r.at[i, k - 1], k
            ).wait_send()
            got = ref.at[source(k)]
            to_peer(got, got, small_s.at[i, k - 1], small_r.at[i, k - 1], k).wait_recv()

    small_wait(0, stats)
    stat = sum(stats[p] for p in range(n)) / full
    stat_h, stat_c = rows_to_lanes(stat[0:1])[:, 0:1], rows_to_lanes(stat[1:2])[:, 0:1]

    def tile_cols(t):
        return slice(t * tile, (t + 1) * tile)

    for t in range(tiles):
        for k in range(1, n):
            part_copy(0, k, t, th, th_in).wait()
            part_copy(1, k, t, tc, tc_in).wait()
        share_h = sum(th_in[k, t].astype(F32) for k in range(n))
        share_c = sum(tc_in[k, t].astype(F32) for k in range(n))
        at = tile_cols(t)
        inv_h, inv_c = inv[0][:, 0:1], inv[1][:, 0:1]
        grad_h = inv_h * (share_h - sh[me, :, at].astype(F32) * inv_h * stat_h)
        grad_c = inv_c * (share_c - sm[me, :, at].astype(F32) * inv_c * stat_c)
        send_h[t] = (left[me, r2:r3, at].astype(F32) + grad_h).astype(BF16)
        mask = jnp.full((rows, tile), dec, jnp.int32) > 0
        send_m[t] = jnp.where(mask, own_tmp[1][:, at].astype(F32) + grad_c, 0.0).astype(BF16)

        @pl.when(s > 0)
        def _():
            section_copy(1, t, send_h.at[t], prev_h.at[0, :, pl.ds(t * tile, tile)], -1).start()
            section_copy(2, t, send_m.at[t], prev_mem.at[0, :, pl.ds(t * tile, tile)], -1).start()

    for t in range(tiles):
        for k in range(1, n):
            part_copy(2, k, t, out, out_in).wait()
        at = tile_cols(t)
        share = sum(out_in[k, t].astype(F32) for k in range(n))
        send_y[t] = (xh[me, :, at].astype(F32) + share).astype(BF16)

        @pl.when(s < sections - 1)
        def _():
            section_copy(3, t, send_y.at[t], next_h.at[0, :, pl.ds(t * tile, tile)], 1).start()

    small_wait(1, sums)
    total = sum(sums[p] for p in range(n))
    row = BETA * row_stat[...] + (1.0 - BETA) * (total[0:1] / (n * cols) + TINY)
    row_new[...] = row
    mean_row = jnp.sum(row, axis=1, keepdims=True) / full
    total_sq = mean_row * jnp.sum(total[1:2] / row, axis=1, keepdims=True)
    root = jnp.sqrt(total_sq / (full * (n * cols)))
    sums[me, 0:1, :] = lax.rsqrt(row) * (jnp.sqrt(mean_row) / jnp.maximum(1.0, root))
    root_col = lax.rsqrt(col)

    def update_body(i, carry):
        at = pl.ds(pl.multiple_of(i * step, step), step)
        factor = rows_to_lanes(sums[me, 0:1, at])[:, 0:1]
        update[0, at, :] = (grad[at, :] * factor * root_col).astype(BF16)
        return carry

    lax.fori_loop(0, full // step, update_body, 0)

    @pl.when(s == 0)
    def _():
        own_tmp[0][...] = jnp.zeros((rows, width), BF16)
        for i, dst in enumerate((next_h, got_mem)):
            pltpu.make_async_copy(own_tmp[0], dst.at[0], local_sem.at[i]).start()
        for i, dst in enumerate((next_h, got_mem)):
            pltpu.make_async_copy(own_tmp[0], dst.at[0], local_sem.at[i]).wait()

    @pl.when(s == sections - 1)
    def _():
        own_tmp[0][...] = jnp.zeros((rows, width), BF16)
        for i, dst in enumerate((prev_h, prev_mem)):
            pltpu.make_async_copy(own_tmp[0], dst.at[0], local_sem.at[i]).start()
        for i, dst in enumerate((prev_h, prev_mem)):
            pltpu.make_async_copy(own_tmp[0], dst.at[0], local_sem.at[i]).wait()

    @pl.when(s < sections - 1)
    def _():
        section_copy(0, 0, fwd_mem.at[0], got_mem.at[0], 1).wait_send()
        for t in range(tiles):
            at = pl.ds(t * tile, tile)
            section_copy(3, t, send_y.at[t], next_h.at[0, :, at], 1).wait_send()
            section_copy(1, t, send_h.at[t], prev_h.at[0, :, at], 1).wait_recv()
            section_copy(2, t, send_m.at[t], prev_mem.at[0, :, at], 1).wait_recv()

    @pl.when(s > 0)
    def _():
        section_copy(0, 0, fwd_mem.at[0], got_mem.at[0], -1).wait_recv()
        for t in range(tiles):
            at = pl.ds(t * tile, tile)
            section_copy(3, t, send_y.at[t], next_h.at[0, :, at], -1).wait_recv()
            section_copy(1, t, send_h.at[t], prev_h.at[0, :, at], -1).wait_send()
            section_copy(2, t, send_m.at[t], prev_mem.at[0, :, at], -1).wait_send()


def finish(
    next_h, got_mem, prev_h, prev_mem, update, row, col, count,
    next_h_out, next_mem_out, prev_h_out, prev_mem_out, update_out, row_out, col_out, sem,
):
    before_dec = lax.axis_index("section") - 1 >= count[0]
    pieces = 4
    size = update.shape[1] // pieces
    pairs = [
        (update.at[0, pl.ds(j * size, size)], update_out.at[0, pl.ds(j * size, size)])
        for j in range(pieces)
    ]
    pairs += [
        (next_h, next_h_out),
        (prev_h, prev_h_out),
        (prev_mem, prev_mem_out),
        (row, row_out),
        (col, col_out),
    ]
    stores = [pltpu.make_async_copy(a, b, sem.at[i]) for i, (a, b) in enumerate(pairs)]
    last = sem.at[len(pairs)]

    @pl.when(before_dec)
    def _():
        pltpu.make_async_copy(got_mem, next_mem_out, last).start()

    @pl.when(jnp.logical_not(before_dec))
    def _():
        pltpu.make_async_copy(next_h, next_mem_out, last).start()

    for store in stores:
        store.start()
    pltpu.make_async_copy(next_h, next_mem_out, last).wait()
    for store in stores:
        store.wait()


def on_device(
    n, sections,
    fwd_h, fwd_mem, saved_h, saved_mem, back_h, back_mem, weight, row_stat, col_stat, enc_count,
    target_embed,
):
    rows, width = fwd_h.shape[1:]
    cols = weight.shape[2]
    full = n * width
    tile = min(256, width)
    tiles = width // tile
    heads = cols // HD
    hbm = pl.BlockSpec(memory_space=pltpu.HBM)
    anywhere = pl.BlockSpec(memory_space=pl.ANY)
    vmem = pl.BlockSpec(memory_space=pltpu.VMEM)
    smem = pl.BlockSpec(memory_space=pltpu.SMEM)
    act = jax.ShapeDtypeStruct((1, rows, width), BF16)
    vact = pltpu.VMEM((1, rows, width), BF16)
    dma = pltpu.SemaphoreType.DMA
    parts = pltpu.VMEM((n, tiles, rows, tile), BF16)
    others = pltpu.VMEM((n - 1, tiles, rows, tile), BF16)
    stored = pltpu.VMEM((n, rows, width), BF16)
    result = pltpu.VMEM((tiles, rows, tile), BF16)
    next_h, got_mem, prev_h, prev_mem, update, row_new, col_new = pl.pallas_call(
        functools.partial(kernel, n, sections, rows, width, cols, tile),
        out_shape=(
            vact, vact, vact, vact,
            pltpu.VMEM((1, full, cols), BF16),
            pltpu.VMEM((1, full), F32),
            pltpu.VMEM((1, cols), F32),
        ),
        in_specs=[hbm] * 7 + [vmem, vmem, smem, hbm],
        out_specs=[vmem] * 7,
        scratch_shapes=[
            pltpu.VMEM((full, cols), BF16),
            stored, stored, stored, stored,
            pltpu.VMEM((4, rows, width), BF16),
            pltpu.VMEM((n, 3 * rows, width), BF16),
            pltpu.VMEM((n, 2 * rows, width), BF16),
            pltpu.VMEM((2 * rows, cols), BF16),
            pltpu.VMEM((heads, rows, rows), F32),
            pltpu.VMEM((3 * rows, cols), BF16),
            pltpu.VMEM((rows, cols), BF16),
            others, others, others, parts, parts, parts,
            pltpu.VMEM((2, rows, 128), F32),
            pltpu.VMEM((n, 8, rows), F32),
            pltpu.VMEM((full, cols), F32),
            pltpu.VMEM((n, 8, full), F32),
            pltpu.VMEM((8, cols), F32),
            result, result, result,
            dma((8,)),
            dma((5, n - 1)), dma((5, n - 1)),
            dma((3, n - 1, tiles)), dma((3, n - 1, tiles)),
            dma((2, n - 1)), dma((2, n - 1)),
            dma((4, tiles)), dma((4, tiles)),
        ],
        compiler_params=pltpu.CompilerParams(
            collective_id=0, has_side_effects=True, vmem_limit_bytes=50 * MIB
        ),
    )(
        fwd_h, fwd_mem, saved_h, saved_mem, back_h, back_mem, weight, row_stat, col_stat,
        enc_count, target_embed,
    )
    return tuple(
        pl.pallas_call(
            finish,
            out_shape=(
                act, act, act, act,
                jax.ShapeDtypeStruct((1, full, cols), BF16),
                jax.ShapeDtypeStruct((1, full), F32),
                jax.ShapeDtypeStruct((1, cols), F32),
            ),
            in_specs=[anywhere] * 7 + [smem],
            out_specs=[hbm] * 7,
            scratch_shapes=[dma((10,))],
            compiler_params=pltpu.CompilerParams(vmem_limit_bytes=MIB),
        )(next_h, got_mem, prev_h, prev_mem, update, row_new, col_new, enc_count)
    )


def solution(mesh):
    act = P("section", None, "dp")
    in_specs = (
        act, act, act, act, act, act, act, P("section", None), P("section", "dp"), P(), P(None, "dp"),
    )
    out_specs = (act, act, act, act, act, P("section", None), P("section", "dp"))
    body = functools.partial(on_device, mesh.shape["dp"], mesh.shape["section"])
    return jax.shard_map(
        body, mesh=mesh, in_specs=in_specs, out_specs=out_specs, check_vma=False
    )
```

```python
import functools

import jax
import jax.numpy as jnp
from jax import lax
from jax.experimental import pallas as pl
from jax.experimental.pallas import tpu as pltpu
from jax.sharding import PartitionSpec as P

HD = 256
EPS = 1e-06
BETA = 0.8
TINY = 1e-30
SCALE = 1.0 / HD**0.5
MESH = pl.DeviceIdType.MESH
F32 = jnp.float32
BF16 = jnp.bfloat16
MIB = 1024 * 1024


def dot_nn(a, b):
    return lax.dot_general(a, b, (((1,), (0,)), ((), ())), preferred_element_type=F32)


def dot_nt(a, b):
    return lax.dot_general(a, b, (((1,), (1,)), ((), ())), preferred_element_type=F32)


def dot_tn(a, b):
    return lax.dot_general(a, b, (((0,), (0,)), ((), ())), preferred_element_type=F32)


def lanes_to_rows(first, second):
    rows = first.shape[0]
    lane = lax.broadcasted_iota(jnp.int32, (rows, 128), 1)
    both = jnp.where(lane == 0, first, second)
    return jnp.transpose(both)[0:2]


def rows_to_lanes(row):
    return jnp.transpose(jnp.broadcast_to(row, (128, row.shape[1])))


def kernel(
    n, sections, rows, width, cols, tile,
    fwd_h, fwd_mem, saved_h, saved_mem, back_h, back_mem, weight, row_stat, col_stat, count, target,
    next_h, got_mem, prev_h, prev_mem, update, row_new, col_new,
    proj, sh, sm, xh, xm, tmp, left, fleft, qkv, probs, right, fmix,
    th, tc, out, th_in, tc_in, out_in, inv, stats, grad, sums, acc, send_h, send_m, send_y,
    hop1, hop2, local_sem, gather_s, gather_r, part_s, part_r, small_s, small_r, sec_s, sec_r,
    hop_s, hop_r,
):
    me = lax.axis_index("dp")
    s = lax.axis_index("section")
    tiles = width // tile
    heads = cols // HD
    full = n * width
    r2, r3 = 2 * rows, 3 * rows
    first_dec = count[0]
    dec = (s >= first_dec).astype(jnp.int32)
    is_first = (s == first_dec).astype(jnp.int32)
    is_last_enc = (s == first_dec - 1).astype(jnp.int32)
    own_tmp = [tmp.at[i] for i in range(4)]
    relayed = n == 2
    quarter = sections // 4
    cut = rows // 2 if relayed else rows
    carries = s < quarter
    base = lax.rem(s, quarter)
    hop_slot = jnp.maximum(s // quarter - 1, 0)

    def when_carrying(f):
        if relayed:
            pl.when(carries)(f)

    def when_carried(f):
        if relayed:
            pl.when(jnp.logical_not(carries))(f)

    def unless_carrying(f):
        if relayed:
            pl.when(jnp.logical_not(carries))(f)
        else:
            f()


    def peer(k):
        return lax.rem(me + k, n)

    def source(k):
        return lax.rem(me + n - k, n)

    loads = [
        (back_h.at[0], own_tmp[0]),
        (back_mem.at[0], own_tmp[1]),
        (fwd_h.at[0], own_tmp[2]),
        (target, own_tmp[3]),
        (saved_h.at[0], sh.at[me]),
        (saved_mem.at[0], sm.at[me]),
        (weight.at[0], proj),
        (fwd_mem.at[0], xm.at[me]),
    ]
    loads = [pltpu.make_async_copy(a, b, local_sem.at[i]) for i, (a, b) in enumerate(loads)]
    for load in loads:
        load.start()

    barrier = pltpu.get_barrier_semaphore()
    for k in range(1, n):
        pl.semaphore_signal(barrier, 1, device_id={"dp": peer(k)}, device_id_type=MESH)

    @pl.when(s > 0)
    def _():
        pl.semaphore_signal(barrier, 1, device_id={"section": s - 1}, device_id_type=MESH)

    @pl.when(s < sections - 1)
    def _():
        pl.semaphore_signal(barrier, 1, device_id={"section": s + 1}, device_id_type=MESH)

    @when_carrying
    def _():
        for j in range(3):
            far = {"section": s + quarter * (j + 1)}
            pl.semaphore_signal(barrier, 1, device_id=far, device_id_type=MESH)

    @when_carried
    def _():
        pl.semaphore_signal(barrier, 1, device_id={"section": base}, device_id_type=MESH)

    ends = (s > 0).astype(jnp.int32) + (s < sections - 1).astype(jnp.int32)
    hops = jnp.where(carries, 3, 1) if relayed else 0
    pl.semaphore_wait(barrier, n - 1 + ends + hops)

    def to_peer(src, dst, send, recv, k):
        return pltpu.make_async_remote_copy(
            src, dst, send, recv, device_id={"dp": peer(k)}, device_id_type=MESH
        )

    def gather_start(i, src, slot):
        for k in range(1, n):
            to_peer(src, slot(me), gather_s.at[i, k - 1], gather_r.at[i, k - 1], k).start()

    def gather_wait(i, src, slot):
        for k in range(1, n):
            to_peer(src, slot(me), gather_s.at[i, k - 1], gather_r.at[i, k - 1], k).wait_send()
            got = slot(source(k))
            to_peer(got, got, gather_s.at[i, k - 1], gather_r.at[i, k - 1], k).wait_recv()

    def g_slot(p):
        return left.at[p, pl.ds(r2, rows)]

    gather_start(0, saved_h.at[0], lambda p: sh.at[p])

    def hop1_copy(j):
        return pltpu.make_async_remote_copy(
            fwd_mem.at[0, pl.ds(rows - cut, cut)], hop1.at[j], hop_s.at[0, 0], hop_r.at[0, j],
            device_id={"section": base}, device_id_type=MESH,
        )

    def hop2_copy(j):
        return to_peer(hop1.at[j], hop2.at[j], hop_s.at[1, j], hop_r.at[1, j], 1)

    def hop3_copy(j):
        return pltpu.make_async_remote_copy(
            hop2.at[j], xm.at[source(1), pl.ds(rows - cut, cut)], hop_s.at[2, j], hop_r.at[2, 0],
            device_id={"section": base + quarter * (j + 1)}, device_id_type=MESH,
        )

    @when_carried
    def _():
        hop1_copy(hop_slot).start()

    def sm_slot(p):
        return sm.at[p]

    def xm_slot(p):
        return xm.at[p, pl.ds(0, cut)]

    xm_own = fwd_mem.at[0, pl.ds(0, cut)]

    @unless_carrying
    def _():
        gather_start(1, saved_mem.at[0], sm_slot)

    def section_copy(i, t, src, dst, by):
        return pltpu.make_async_remote_copy(
            src, dst, sec_s.at[i, t], sec_r.at[i, t],
            device_id={"section": s + by}, device_id_type=MESH,
        )

    @pl.when(s < sections - 1)
    def _():
        section_copy(0, 0, fwd_mem.at[0], got_mem.at[0], 1).start()

    def select(flag, yes, no, dst):
        step = 32

        def body(i, carry):
            at = pl.ds(pl.multiple_of(i * step, step), step)
            mask = jnp.full((step, width), flag, jnp.int32) > 0
            dst[at, :] = jnp.where(mask, yes[at, :].astype(F32), no[at, :].astype(F32)).astype(BF16)
            return carry

        lax.fori_loop(0, rows // step, body, 0)

    for i in range(4):
        loads[i].wait()
    select(is_last_enc, own_tmp[1], own_tmp[0], left.at[me, pl.ds(r2, rows)])
    select(is_first, own_tmp[3], own_tmp[2], xh.at[me])

    def normalize(h_ref, m_ref, dst, keep):
        step = 32

        def body(i, carry):
            at = pl.ds(pl.multiple_of(i * step, step), step)
            at_c = pl.ds(pl.multiple_of(rows + i * step, step), step)
            h = [h_ref[p, at, :].astype(F32) for p in range(n)]
            mask = jnp.full((step, width), dec, jnp.int32) > 0
            c = [jnp.where(mask, m_ref[p, at, :].astype(F32), h[p]) for p in range(n)]
            for j, (v, where) in enumerate(((h, at), (c, at_c))):
                total = sum(jnp.sum(x * x, axis=1, keepdims=True) for x in v)
                r = lax.rsqrt(total / full + EPS)
                for p in range(n):
                    dst[p, where, :] = (v[p] * r).astype(BF16)
                if keep:
                    inv[j, at, :] = jnp.broadcast_to(r, (step, 128))
            return carry

        lax.fori_loop(0, rows // step, body, 0)

    def head_cols(h):
        return pl.ds(pl.multiple_of(h * HD, HD), HD)

    def project(src, lo, size, at):
        return sum(
            dot_nn(src[p, lo : lo + size, :], proj[p * width : (p + 1) * width, at])
            for p in range(n)
        )

    def softmax(q, kv):
        score = dot_nt(q, kv) * SCALE
        e = jnp.exp(score - jnp.max(score, axis=1, keepdims=True))
        return e / jnp.sum(e, axis=1, keepdims=True)

    loads[4].wait()
    loads[5].wait()
    gather_wait(0, saved_h.at[0], lambda p: sh.at[p])

    @when_carrying
    def _():
        for j in range(3):
            hop1_copy(j).wait_recv()
            hop2_copy(j).start()

    gather_start(2, g_slot(me), g_slot)

    @unless_carrying
    def _():
        gather_wait(1, saved_mem.at[0], sm_slot)

    gather_start(3, xh.at[me], lambda p: xh.at[p])
    normalize(sh, sm, left, True)
    loads[6].wait()

    def attend_body(h, carry):
        at = head_cols(h)
        both = project(left, 0, r2, at).astype(BF16)
        qkv[:, at] = both
        q, kv = both[:rows], both[rows:]
        p = softmax(q, kv)
        probs[h] = p
        right[r2:r3, at] = dot_nn(p.astype(BF16), kv).astype(BF16)
        return carry

    lax.fori_loop(0, heads, attend_body, 0)

    @when_carrying
    def _():
        for j in range(3):
            hop2_copy(j).wait_recv()
            hop3_copy(j).start()

    gather_wait(2, g_slot(me), g_slot)

    @unless_carrying
    def _():
        gather_start(4, xm_own, xm_slot)


    def back_body(h, carry):
        stat_q, stat_k = carry
        at = head_cols(h)
        dmix = project(left, r2, rows, at).astype(BF16)
        q, kv = qkv[0:rows, at], qkv[rows:r2, at]
        p = probs[h]
        dprobs = dot_nt(dmix, kv)
        dval = dot_tn(p.astype(BF16), dmix)
        inner = jnp.sum(dprobs * p, axis=1, keepdims=True)
        dscore = (p * (dprobs - inner) * SCALE).astype(BF16)
        dq = dot_nn(dscore, kv).astype(BF16)
        dkv = (dot_tn(dscore, q) + dval).astype(BF16)
        right[0:rows, at] = dq
        right[rows:r2, at] = dkv
        stat_q += jnp.sum(dq.astype(F32) * q.astype(F32), axis=1, keepdims=True)
        stat_k += jnp.sum(dkv.astype(F32) * kv.astype(F32), axis=1, keepdims=True)
        return stat_q, stat_k

    zero_col = jnp.zeros((rows, 1), F32)
    stat_q, stat_k = lax.fori_loop(0, heads, back_body, (zero_col, zero_col))
    decf = jnp.full((rows, 1), dec, jnp.int32).astype(F32)
    stats[me] = lanes_to_rows(stat_q + (1.0 - decf) * stat_k, decf * stat_k)
    for k in range(1, n):
        to_peer(stats.at[me], stats.at[me], small_s.at[0, k - 1], small_r.at[0, k - 1], k).start()

    def row_tile(p, t):
        return pl.ds(pl.multiple_of(p * width + t * tile, tile), tile)

    def terms(p, t, to_h, to_c):
        both = dot_nt(right[0:r2, :], proj[row_tile(p, t), :])
        bq, bk = both[:rows], both[rows:]
        flag = jnp.full((rows, tile), dec, jnp.int32).astype(F32)
        to_h[...] = (bq + (1.0 - flag) * bk).astype(BF16)
        to_c[...] = (flag * bk).astype(BF16)

    def part_copy(i, k, t, src, dst):
        return to_peer(
            src.at[k - 1, t], dst.at[k, t], part_s.at[i, k - 1, t], part_r.at[i, k - 1, t], k
        )

    for k in range(1, n):
        for t in range(tiles):
            terms(peer(k), t, th.at[k - 1, t], tc.at[k - 1, t])
            part_copy(0, k, t, th, th_in).start()

            @unless_carrying
            def _():
                part_copy(1, k, t, tc, tc_in).start()


    def own_terms(t, carry):
        terms(me, t, th_in.at[0, t], tc_in.at[0, t])
        return carry

    lax.fori_loop(0, tiles, own_terms, 0)

    loads[7].wait()
    gather_wait(3, xh.at[me], lambda p: xh.at[p])

    @unless_carrying
    def _():
        gather_wait(4, xm_own, xm_slot)

    @when_carried
    def _():
        hop3_copy(hop_slot).wait_recv()

    normalize(xh, xm, fleft, False)

    def forward_body(h, carry):
        at = head_cols(h)
        both = project(fleft, 0, r2, at).astype(BF16)
        kv = both[rows:]
        p = softmax(both[:rows], kv).astype(BF16)
        fmix[:, at] = dot_nn(p, kv).astype(BF16)
        return carry

    lax.fori_loop(0, heads, forward_body, 0)
    for k in range(1, n):
        for t in range(tiles):
            out[k - 1, t] = dot_nt(fmix[...], proj[row_tile(peer(k), t), :]).astype(BF16)
            part_copy(2, k, t, out, out_in).start()

    def own_out(t, carry):
        out_in[0, t] = dot_nt(fmix[...], proj[row_tile(me, t), :]).astype(BF16)
        return carry

    lax.fori_loop(0, tiles, own_out, 0)

    acc[...] = jnp.zeros_like(acc)

    def grad_body(f, carry):
        p, t = f // tiles, f % tiles
        tl = left[p, :, pl.ds(pl.multiple_of(t * tile, tile), tile)]
        g = dot_tn(tl, right[...])
        grad[pl.ds(pl.multiple_of(f * tile, tile), tile), :] = g
        acc[...] += jnp.sum((g * g).reshape(tile // 8, 8, cols), axis=0)
        return carry

    lax.fori_loop(0, n * tiles, grad_body, 0)
    col = BETA * col_stat[...] + (1.0 - BETA) * (
        jnp.sum(acc[...], axis=0, keepdims=True) / full + TINY
    )
    col_new[...] = col
    inv_col = 1.0 / col

    step = 128

    def sums_body(i, carry):
        at = pl.ds(pl.multiple_of(i * step, step), step)
        g = grad[at, :]
        g = g * g
        sums[me, :, at] = lanes_to_rows(
            jnp.sum(g, axis=1, keepdims=True), jnp.sum(g * inv_col, axis=1, keepdims=True)
        )
        return carry

    lax.fori_loop(0, full // step, sums_body, 0)
    for k in range(1, n):
        to_peer(sums.at[me], sums.at[me], small_s.at[1, k - 1], small_r.at[1, k - 1], k).start()

    def small_wait(i, ref):
        for k in range(1, n):
            to_peer(
                ref.at[me], ref.at[me], small_s.at[i, k - 1], small_r.at[i, k - 1], k
            ).wait_send()
            got = ref.at[source(k)]
            to_peer(got, got, small_s.at[i, k - 1], small_r.at[i, k - 1], k).wait_recv()

    small_wait(0, stats)
    stat = sum(stats[p] for p in range(n)) / full
    stat_h, stat_c = rows_to_lanes(stat[0:1])[:, 0:1], rows_to_lanes(stat[1:2])[:, 0:1]

    def tile_cols(t):
        return slice(t * tile, (t + 1) * tile)

    for t in range(tiles):
        for k in range(1, n):
            part_copy(0, k, t, th, th_in).wait()

            @unless_carrying
            def _():
                part_copy(1, k, t, tc, tc_in).wait()

        share_h = sum(th_in[k, t].astype(F32) for k in range(n))
        share_c = sum(tc_in[k, t].astype(F32) for k in range(n))
        at = tile_cols(t)
        inv_h, inv_c = inv[0][:, 0:1], inv[1][:, 0:1]
        grad_h = inv_h * (share_h - sh[me, :, at].astype(F32) * inv_h * stat_h)
        grad_c = inv_c * (share_c - sm[me, :, at].astype(F32) * inv_c * stat_c)
        send_h[t] = (left[me, r2:r3, at].astype(F32) + grad_h).astype(BF16)
        mask = jnp.full((rows, tile), dec, jnp.int32) > 0
        send_m[t] = jnp.where(mask, own_tmp[1][:, at].astype(F32) + grad_c, 0.0).astype(BF16)

        @pl.when(s > 0)
        def _():
            section_copy(1, t, send_h.at[t], prev_h.at[0, :, pl.ds(t * tile, tile)], -1).start()
            section_copy(2, t, send_m.at[t], prev_mem.at[0, :, pl.ds(t * tile, tile)], -1).start()

    for t in range(tiles):
        for k in range(1, n):
            part_copy(2, k, t, out, out_in).wait()
        at = tile_cols(t)
        share = sum(out_in[k, t].astype(F32) for k in range(n))
        send_y[t] = (xh[me, :, at].astype(F32) + share).astype(BF16)

        @pl.when(s < sections - 1)
        def _():
            section_copy(3, t, send_y.at[t], next_h.at[0, :, pl.ds(t * tile, tile)], 1).start()

    small_wait(1, sums)
    total = sum(sums[p] for p in range(n))
    row = BETA * row_stat[...] + (1.0 - BETA) * (total[0:1] / (n * cols) + TINY)
    row_new[...] = row
    mean_row = jnp.sum(row, axis=1, keepdims=True) / full
    total_sq = mean_row * jnp.sum(total[1:2] / row, axis=1, keepdims=True)
    root = jnp.sqrt(total_sq / (full * (n * cols)))
    sums[me, 0:1, :] = lax.rsqrt(row) * (jnp.sqrt(mean_row) / jnp.maximum(1.0, root))
    root_col = lax.rsqrt(col)

    def update_body(i, carry):
        at = pl.ds(pl.multiple_of(i * step, step), step)
        factor = rows_to_lanes(sums[me, 0:1, at])[:, 0:1]
        update[0, at, :] = (grad[at, :] * factor * root_col).astype(BF16)
        return carry

    lax.fori_loop(0, full // step, update_body, 0)

    @when_carried
    def _():
        hop1_copy(hop_slot).wait_send()

    @when_carrying
    def _():
        for j in range(3):
            hop2_copy(j).wait_send()
            hop3_copy(j).wait_send()

    @pl.when(s == 0)
    def _():
        own_tmp[0][...] = jnp.zeros((rows, width), BF16)
        for i, dst in enumerate((next_h, got_mem)):
            pltpu.make_async_copy(own_tmp[0], dst.at[0], local_sem.at[i]).start()
        for i, dst in enumerate((next_h, got_mem)):
            pltpu.make_async_copy(own_tmp[0], dst.at[0], local_sem.at[i]).wait()

    @pl.when(s == sections - 1)
    def _():
        own_tmp[0][...] = jnp.zeros((rows, width), BF16)
        for i, dst in enumerate((prev_h, prev_mem)):
            pltpu.make_async_copy(own_tmp[0], dst.at[0], local_sem.at[i]).start()
        for i, dst in enumerate((prev_h, prev_mem)):
            pltpu.make_async_copy(own_tmp[0], dst.at[0], local_sem.at[i]).wait()

    @pl.when(s < sections - 1)
    def _():
        section_copy(0, 0, fwd_mem.at[0], got_mem.at[0], 1).wait_send()
        for t in range(tiles):
            at = pl.ds(t * tile, tile)
            section_copy(3, t, send_y.at[t], next_h.at[0, :, at], 1).wait_send()
            section_copy(1, t, send_h.at[t], prev_h.at[0, :, at], 1).wait_recv()
            section_copy(2, t, send_m.at[t], prev_mem.at[0, :, at], 1).wait_recv()

    @pl.when(s > 0)
    def _():
        section_copy(0, 0, fwd_mem.at[0], got_mem.at[0], -1).wait_recv()
        for t in range(tiles):
            at = pl.ds(t * tile, tile)
            section_copy(3, t, send_y.at[t], next_h.at[0, :, at], -1).wait_recv()
            section_copy(1, t, send_h.at[t], prev_h.at[0, :, at], -1).wait_send()
            section_copy(2, t, send_m.at[t], prev_mem.at[0, :, at], -1).wait_send()


def finish(
    next_h, got_mem, prev_h, prev_mem, update, row, col, count,
    next_h_out, next_mem_out, prev_h_out, prev_mem_out, update_out, row_out, col_out, sem,
):
    before_dec = lax.axis_index("section") - 1 >= count[0]
    pieces = 4
    size = update.shape[1] // pieces
    pairs = [
        (update.at[0, pl.ds(j * size, size)], update_out.at[0, pl.ds(j * size, size)])
        for j in range(pieces)
    ]
    pairs += [
        (next_h, next_h_out),
        (prev_h, prev_h_out),
        (prev_mem, prev_mem_out),
        (row, row_out),
        (col, col_out),
    ]
    stores = [pltpu.make_async_copy(a, b, sem.at[i]) for i, (a, b) in enumerate(pairs)]
    last = sem.at[len(pairs)]

    @pl.when(before_dec)
    def _():
        pltpu.make_async_copy(got_mem, next_mem_out, last).start()

    @pl.when(jnp.logical_not(before_dec))
    def _():
        pltpu.make_async_copy(next_h, next_mem_out, last).start()

    for store in stores:
        store.start()
    pltpu.make_async_copy(next_h, next_mem_out, last).wait()
    for store in stores:
        store.wait()


def on_device(
    n, sections,
    fwd_h, fwd_mem, saved_h, saved_mem, back_h, back_mem, weight, row_stat, col_stat, enc_count,
    target_embed,
):
    rows, width = fwd_h.shape[1:]
    cols = weight.shape[2]
    full = n * width
    tile = min(256, width)
    tiles = width // tile
    heads = cols // HD
    hbm = pl.BlockSpec(memory_space=pltpu.HBM)
    anywhere = pl.BlockSpec(memory_space=pl.ANY)
    vmem = pl.BlockSpec(memory_space=pltpu.VMEM)
    smem = pl.BlockSpec(memory_space=pltpu.SMEM)
    act = jax.ShapeDtypeStruct((1, rows, width), BF16)
    vact = pltpu.VMEM((1, rows, width), BF16)
    dma = pltpu.SemaphoreType.DMA
    parts = pltpu.VMEM((n, tiles, rows, tile), BF16)
    others = pltpu.VMEM((n - 1, tiles, rows, tile), BF16)
    stored = pltpu.VMEM((n, rows, width), BF16)
    result = pltpu.VMEM((tiles, rows, tile), BF16)
    next_h, got_mem, prev_h, prev_mem, update, row_new, col_new = pl.pallas_call(
        functools.partial(kernel, n, sections, rows, width, cols, tile),
        out_shape=(
            vact, vact, vact, vact,
            pltpu.VMEM((1, full, cols), BF16),
            pltpu.VMEM((1, full), F32),
            pltpu.VMEM((1, cols), F32),
        ),
        in_specs=[hbm] * 7 + [vmem, vmem, smem, hbm],
        out_specs=[vmem] * 7,
        scratch_shapes=[
            pltpu.VMEM((full, cols), BF16),
            stored, stored, stored, stored,
            pltpu.VMEM((4, rows, width), BF16),
            pltpu.VMEM((n, 3 * rows, width), BF16),
            pltpu.VMEM((n, 2 * rows, width), BF16),
            pltpu.VMEM((2 * rows, cols), BF16),
            pltpu.VMEM((heads, rows, rows), F32),
            pltpu.VMEM((3 * rows, cols), BF16),
            pltpu.VMEM((rows, cols), BF16),
            others, others, others, parts, parts, parts,
            pltpu.VMEM((2, rows, 128), F32),
            pltpu.VMEM((n, 2, rows), F32),
            pltpu.VMEM((full, cols), F32),
            pltpu.VMEM((n, 2, full), F32),
            pltpu.VMEM((8, cols), F32),
            result, result, result,
            pltpu.VMEM((3, rows // 2, width), BF16),
            pltpu.VMEM((3, rows // 2, width), BF16),
            dma((8,)),
            dma((5, n - 1)), dma((5, n - 1)),
            dma((3, n - 1, tiles)), dma((3, n - 1, tiles)),
            dma((2, n - 1)), dma((2, n - 1)),
            dma((4, tiles)), dma((4, tiles)),
            dma((3, 3)), dma((3, 3)),
        ],
        compiler_params=pltpu.CompilerParams(
            collective_id=0, has_side_effects=True, vmem_limit_bytes=50 * MIB
        ),
    )(
        fwd_h, fwd_mem, saved_h, saved_mem, back_h, back_mem, weight, row_stat, col_stat,
        enc_count, target_embed,
    )
    return tuple(
        pl.pallas_call(
            finish,
            out_shape=(
                act, act, act, act,
                jax.ShapeDtypeStruct((1, full, cols), BF16),
                jax.ShapeDtypeStruct((1, full), F32),
                jax.ShapeDtypeStruct((1, cols), F32),
            ),
            in_specs=[anywhere] * 7 + [smem],
            out_specs=[hbm] * 7,
            scratch_shapes=[dma((10,))],
            compiler_params=pltpu.CompilerParams(vmem_limit_bytes=MIB),
        )(next_h, got_mem, prev_h, prev_mem, update, row_new, col_new, enc_count)
    )


def solution(mesh):
    act = P("section", None, "dp")
    in_specs = (
        act, act, act, act, act, act, act, P("section", None), P("section", "dp"), P(), P(None, "dp"),
    )
    out_specs = (act, act, act, act, act, P("section", None), P("section", "dp"))
    body = functools.partial(on_device, mesh.shape["dp"], mesh.shape["section"])
    return jax.shard_map(
        body, mesh=mesh, in_specs=in_specs, out_specs=out_specs, check_vma=False
    )
```
